256 devices in a mesh: obs: 64 (over z, y, core), blk: 4 (over x).
Axes of the slice: x: 4, y: 4, z: 8, core: 2. Of those that a mesh axis runs over, the one named last changes fastest.
Arguments:
- jac_cols: float32 [2048, 262144], P('obs', 'blk'), may hold values from -6 to 6
- obs_group: int32 [4, 65536], P('blk', 'obs'), may hold values from 0 to 15
- group_weight: float32 [16], replicated, may hold values from 0.3 to 3
- pattern: int32 [4, 64, 16], P('blk', 'obs'), may hold values from 0 to 1, as said below
- pairs: int32 [128, 2], replicated, may hold values from 0 to 15, as said below
Outputs:
- normal: float32 [128, 128, 128], P('obs', 'blk')
The draws below stay inside these ranges and needn't reach their ends.
Inputs may be any that keep to these rules, and one draw needn't show every extreme that they name: `pattern`: every panel marks between 2 and 16 blocks; in every draw some panel marks all 16. Distinct pairs, each with first entry <= second entry.
All inputs are finite; a program needn't handle non-finite values.
Results may differ from the reference program's by a relative error of at most 0.0003.
Values sent between devices are 32-bit elements; how exact they have to be, the bound alone decides.
No kernel may reach another device: no remote copies, remote signals or barrier semaphores. Data moves between devices by JAX's collectives and lax.ppermute only.
A program may use at most 128 MiB of HBM per device.

```python
import math
import jax
import jax.numpy as jnp
import numpy as np
from jax import lax

BS = 128
NB = 16
OBS_DEV = 1024
GROUPS = 16
COLS = 2048
OBS = 262144
NPAIR = 128
N_OBS = 64
N_BLK = 4


def draw_pattern(key, part):
    panels = N_BLK * N_OBS
    key_count = jax.random.fold_in(key, 11)
    key_rank = jax.random.fold_in(key, 12)
    key_full = jax.random.fold_in(key, 13)
    counts = jax.random.randint(key_count, (panels,), 2, NB + 1)
    full_at = jax.random.randint(key_full, (), 0, panels)
    counts = jnp.where(jnp.arange(panels) == full_at, NB, counts)
    ranks = jax.vmap(lambda sub: jax.random.permutation(sub, NB))(jax.random.split(key_rank, panels))
    marks = (ranks < counts[:, None]).astype(jnp.int32)
    return marks.reshape(N_BLK, N_OBS, NB)


def draw_pairs(key, part):
    rows_tab, cols_tab = np.triu_indices(NB)
    rows_tab = jnp.asarray(rows_tab, jnp.int32)
    cols_tab = jnp.asarray(cols_tab, jnp.int32)
    chosen = jax.random.permutation(jax.random.fold_in(key, 21), NB * (NB + 1) // 2)[:NPAIR]
    return jnp.stack([rows_tab[chosen], cols_tab[chosen]], axis=1).astype(jnp.int32)


def touch_ends(entries, stream_key, least, high):
    shape = entries.shape
    spot = [jax.random.randint(jax.random.fold_in(stream_key, axis), (), 0, shape[axis]) for axis in range(len(shape))]
    entries = entries.at[tuple(spot)].set(least)
    longest = shape.index(max(shape))
    spot[longest] = (spot[longest] + 1) % shape[longest]
    return entries.at[tuple(spot)].set(high)


def steps_of(own_key, extent, pieces, least, top_value):
    level, own = 1.0, jax.random.fold_in(own_key, 6)
    for axis_at, parts in pieces:
        draws = jnp.exp(jax.random.uniform(jax.random.fold_in(own, axis_at), (parts,), jnp.float32, least / len(pieces), top_value / len(pieces)))
        level = level * jnp.repeat(draws, extent[axis_at] // parts).reshape([-1 if axis == axis_at else 1 for axis in range(len(extent))])
    return level


def centred(rng, shape, deviation, bound, shards=(), kind=jnp.bfloat16):
    result = deviation * jax.random.normal(rng, shape, jnp.float32)
    if shards:
        result = result * steps_of(rng, shape, shards, -0.22, 0.18)
    return jnp.clip(result, -bound, bound).astype(kind)


def setup_inputs(seed: int = 0) -> dict:
    keys = jax.random.split(jax.random.key(seed), 6)
    return {
        "jac_cols": centred(keys[0], (COLS, OBS), 1.0, 6.0, ((0, 64), (1, 4)), jnp.float32),
        "obs_group": touch_ends(jax.random.randint(keys[1], (N_BLK, OBS // N_BLK), 0, GROUPS), jax.random.fold_in(keys[1], 1), 0, GROUPS - 1).astype(jnp.int32),
        "group_weight": jnp.clip(jnp.exp(jax.random.uniform(keys[2], (GROUPS,), jnp.float32, math.log(0.3), math.log(3.0))), 0.3, 3.0),
        "pattern": draw_pattern(jax.random.fold_in(keys[5], 71), 0),
        "pairs": draw_pairs(jax.random.fold_in(keys[5], 71), 0),
    }


def reference(jac_cols, obs_group, group_weight, pattern, pairs):
    panels = N_BLK * N_OBS
    weights = (group_weight * group_weight)[obs_group.reshape(-1)]
    flat = pattern.reshape(panels, NB).astype(jnp.float32)
    scale = 1.0 / math.sqrt(OBS)
    first = pairs[:, 0]
    second = pairs[:, 1]

    def one_panel(total, panel):
        start = (panel * OBS_DEV).astype(jnp.int32)
        block = lax.dynamic_slice_in_dim(jac_cols, start, OBS_DEV, 1)
        wrow = lax.dynamic_slice_in_dim(weights, start, OBS_DEV, 0)
        jblocks = block.reshape(NB, BS, OBS_DEV)
        wblocks = (block * wrow[None, :]).reshape(NB, BS, OBS_DEV)
        marks = flat[panel]
        tiles = jnp.einsum('pao,pbo->pab', jblocks[first], wblocks[second], precision=lax.Precision.HIGHEST)
        factor = marks[first] * marks[second] * scale
        return (total + tiles * factor[:, None, None], None)
    start_total = jnp.zeros((NPAIR, BS, BS), jnp.float32)
    total, _ = lax.scan(one_panel, start_total, jnp.arange(panels, dtype=jnp.int32))
    return total
```

```python
import math

import jax
import jax.numpy as jnp
import numpy as np
from jax import lax
from jax.experimental import pallas as pl
from jax.experimental.pallas import tpu as pltpu
from jax.sharding import Mesh, PartitionSpec as P

NZ, NY, NC, NX = 8, 4, 2, 4
OBS_AXES = ("z", "y", "c")
VMEM_LIMIT = 60 * 1024 * 1024


def relayout(jac):
    rows, total = jac.shape
    parts = NZ * NY * NC
    width = total // parts
    step = NY * NC

    def body(src, dst):
        for s in range(step):
            dst[s] = src[:, s * width:(s + 1) * width]

    return pl.pallas_call(
        body,
        grid=(parts // step,),
        in_specs=[pl.BlockSpec((rows, step * width), lambda i: (0, i))],
        out_specs=pl.BlockSpec((step, rows, width), lambda i: (i, 0, 0)),
        out_shape=jax.ShapeDtypeStruct((parts, rows, width), jac.dtype),
        name="relayout",
    )(jac)


def super_tiles(groups, zs, info, factors):
    count = len(groups)
    width = groups[0].shape[-1]
    pairs = info["pairs"]
    npair = len(pairs)
    first = jnp.stack([zs[a] for a, _ in pairs])
    second = jnp.stack([zs[b] for _, b in pairs])
    slot_a = jnp.array([a for a, _ in pairs], jnp.int32)
    slot_b = jnp.array([b for _, b in pairs], jnp.int32)
    swap = first > second
    rows = jnp.where(swap, slot_b, slot_a)
    cols = jnp.where(swap, slot_a, slot_b)
    core = lax.axis_index("c").astype(jnp.int32).reshape(1)

    def body(rows_ref, cols_ref, core_ref, *refs):
        srcs = refs[:count]
        fac = refs[count]
        keep, give = refs[count + 1:count + 3]
        high, low, acc = refs[count + 3:]
        step = pl.program_id(0)

        @pl.when(step == 0)
        def _():
            for g in range(count):

                def split(s, carry, g=g):
                    half = s // (NY * NC // 2)
                    value = srcs[g][s] * fac[pl.ds(2 * g + half, 1), :]
                    top = value.astype(jnp.bfloat16)
                    rest = (value - top.astype(jnp.float32)).astype(jnp.bfloat16)
                    start = pl.multiple_of(s * 32, 32)
                    high[g, pl.ds(start, 32), :] = top
                    low[g, pl.ds(start, 32), :] = rest
                    return carry

                lax.fori_loop(0, NY * NC, split, 0)

        a = rows_ref[step]
        b = cols_ref[step]

        def dot(u, v):
            return lax.dot_general(
                u, v, (((1,), (1,)), ((), ())), preferred_element_type=jnp.float32
            )

        ha, hb = high[a], high[b]
        acc[...] = dot(ha, hb) + (dot(ha, low[b]) + dot(low[a], hb))
        mine = core_ref[0]
        for x in range(NX):
            for y in range(NY):
                at = x * 32 + y * 8
                own = pl.multiple_of(mine * 128 + at, 8)
                other = pl.multiple_of((1 - mine) * 128 + at, 8)
                for h in range(2):
                    lanes = slice(h * 128, (h + 1) * 128)
                    keep[y, x, 0, h] = acc[pl.ds(own, 8), lanes]
                    give[y, x, 0, h] = acc[pl.ds(other, 8), lanes]

    shape = (NY, NX, npair, 2, 8, 128)
    block = pl.BlockSpec((NY, NX, 1, 2, 8, 128), lambda p, *_: (0, 0, p, 0, 0, 0))
    whole = pl.BlockSpec((NY * NC, 32, width), lambda p, *_: (0, 0, 0))
    return pl.pallas_call(
        body,
        grid_spec=pltpu.PrefetchScalarGridSpec(
            num_scalar_prefetch=3,
            grid=(npair,),
            in_specs=[whole] * count
            + [pl.BlockSpec((2 * count, width), lambda p, *_: (0, 0))],
            out_specs=[block, block],
            scratch_shapes=[
                pltpu.VMEM((count, 256, width), jnp.bfloat16),
                pltpu.VMEM((count, 256, width), jnp.bfloat16),
                pltpu.VMEM((256, 256), jnp.float32),
            ],
        ),
        out_shape=[jax.ShapeDtypeStruct(shape, jnp.float32)] * 2,
        compiler_params=pltpu.CompilerParams(vmem_limit_bytes=VMEM_LIMIT),
        cost_estimate=pl.CostEstimate(
            flops=npair * 256 * 256 * width * 6,
            bytes_accessed=count * 256 * width * 4 + npair * 256 * 256 * 4,
            transcendentals=0,
        ),
        name="super_tiles",
    )(rows, cols, core, *groups, factors)


def swap_cores(value):
    return lax.ppermute(value, "c", [(0, 1), (1, 0)])


def reduce_rows(keep, give):
    total = keep + swap_cores(give)
    parts = total.reshape(NY * NX, -1, 8, 128)
    return lax.all_to_all(parts, ("y", "x"), 0, 0, tiled=True)


def gather_tiles(parts, index, valid):
    sizes = [p.shape[1] for p in parts]
    count = index.shape[0]

    def body(index_ref, valid_ref, *refs):
        srcs = refs[:len(parts)]
        out, sums = refs[len(parts):]
        base = 0
        for src, size in zip(srcs, sizes):

            def add(t, carry, src=src, base=base):
                value = src[0, t]
                for s in range(1, NY * NX):
                    value = value + src[s, t]
                sums[base + t] = value
                return carry

            lax.fori_loop(0, size, add, 0)
            base += size

        def pick(k, carry):
            value = sums[index_ref[k]]
            out[k] = jnp.where(valid_ref[k] > 0, value, 0.0)
            return carry

        lax.fori_loop(0, count, pick, 0)

    return pl.pallas_call(
        body,
        grid_spec=pltpu.PrefetchScalarGridSpec(
            num_scalar_prefetch=2,
            grid=(1,),
            in_specs=[pl.BlockSpec(p.shape, lambda i, *_: (0, 0, 0, 0)) for p in parts],
            out_specs=pl.BlockSpec((count, 8, 128), lambda i, *_: (0, 0, 0)),
            scratch_shapes=[pltpu.VMEM((sum(sizes), 8, 128), jnp.float32)],
        ),
        out_shape=jax.ShapeDtypeStruct((count, 8, 128), jnp.float32),
        compiler_params=pltpu.CompilerParams(vmem_limit_bytes=VMEM_LIMIT),
        name="gather_tiles",
    )(index, valid, *parts)


def on_device(jac, obs_group, group_weight, pattern, pairs):
    count = pairs.shape[0]
    total_obs = jac.shape[1] * NX
    message = relayout(jac)
    received = lax.all_to_all(message, OBS_AXES, 0, 0, tiled=True)
    groups = [received[g * NY * NC:(g + 1) * NY * NC] for g in range(NZ)]
    zs = [jnp.int32(g) for g in range(NZ)]

    choice = obs_group[0][None, :] == jnp.arange(group_weight.shape[0], dtype=jnp.int32)[:, None]
    root = jnp.sum(jnp.where(choice, group_weight[:, None], 0.0), axis=0)
    factors = pattern[0, 0].astype(jnp.float32)[:, None] * root[None, :]

    listed = [(a, b) for a in range(NZ) for b in range(a, NZ)]
    table = np.zeros((NZ, NZ), np.int32)
    for at, (a, b) in enumerate(listed):
        table[a, b] = table[b, a] = at
    keep, give = super_tiles(groups, zs, {"pairs": listed}, factors)
    part = reduce_rows(keep, give)

    first, second = pairs[:, 0], pairs[:, 1]
    place = jnp.asarray(table)[first // 2, second // 2] * 2 + second % 2
    valid = (first % 2 == lax.axis_index("c")).astype(jnp.int32)
    tiles = gather_tiles([part], place, valid)
    owned = lax.all_to_all(
        tiles.reshape(NZ * NY * NC, count // (NZ * NY * NC), 8, 128), OBS_AXES, 0, 0, tiled=True
    )
    owned = owned.reshape(NZ, NY, NC, -1, 8, 128)
    result = jnp.sum(owned, axis=(0, 2)) * (1.0 / math.sqrt(total_obs))
    return result.transpose(1, 0, 2, 3).reshape(-1, NY * 8, 128)


def solution(mesh):
    fine = Mesh(mesh.devices.reshape(NZ, NY, NC, NX), ("z", "y", "c", "x"))
    return jax.shard_map(
        on_device,
        mesh=fine,
        in_specs=(P(OBS_AXES, "x"), P("x", OBS_AXES), P(), P("x", OBS_AXES, None), P()),
        out_specs=P(OBS_AXES, "x", None),
        check_vma=False,
    )
```

```python
import math

import jax
import jax.numpy as jnp
from jax import lax
from jax.experimental import pallas as pl
from jax.experimental.pallas import tpu as pltpu
from jax.sharding import Mesh, PartitionSpec as P

NZ, NY, NC, NX = 8, 4, 2, 4
PARTS = NZ * NY * NC
OBS_AXES = ("z", "y", "c")
NB, BS = 16, 128
OWNERS = 4
EARLY, LATE = 24, 8
EA, LA = OWNERS * EARLY, OWNERS * LATE
VMEM_LIMIT = 60 * 1024 * 1024
SMALL = pl.CostEstimate(flops=1, bytes_accessed=1, transcendentals=0)
PARAMS = pltpu.CompilerParams(vmem_limit_bytes=VMEM_LIMIT)
ANYWHERE = pl.BlockSpec(memory_space=pl.ANY)


def relayout(jac, start, rows):
    width = jac.shape[1] // PARTS

    def body(src, out, hold, sems):
        loads, stores = [], []
        for i in range(PARTS):
            part = src.at[pl.ds(start, rows), pl.ds(i * width, width)]
            loads.append(pltpu.make_async_copy(part, hold.at[i], sems.at[0, i]))
            stores.append(pltpu.make_async_copy(hold.at[i], out.at[i], sems.at[1, i]))
        for load in loads:
            load.start()
        for load, store in zip(loads, stores):
            load.wait()
            store.start()
        for store in stores:
            store.wait()

    shape = (PARTS, rows, width)
    return pl.pallas_call(
        body,
        in_specs=[ANYWHERE],
        out_specs=ANYWHERE,
        out_shape=jax.ShapeDtypeStruct(shape, jac.dtype),
        scratch_shapes=[pltpu.VMEM(shape, jac.dtype), pltpu.SemaphoreType.DMA((2, PARTS))],
        compiler_params=PARAMS,
        cost_estimate=SMALL,
        name="relayout",
    )(jac)


def dot(u, v):
    return lax.dot_general(u, v, (((1,), (1,)), ((), ())), preferred_element_type=jnp.float32)


def split(value):
    top = value.astype(jnp.bfloat16)
    return top, (value - top.astype(jnp.float32)).astype(jnp.bfloat16)


def each_pair(pairs_ref, mine, store):
    def one(s, carry):
        z, y, w = s // (NY * 2), (s // 2) % NY, s % 2
        k = ((z * NY + y) * NC + mine) * 2 + w
        store(y, z * 2 + w, pairs_ref[2 * k], pairs_ref[2 * k + 1])
        return carry

    lax.fori_loop(0, NZ * NY * 2, one, 0, unroll=8)


def early_tiles(received, factors, pairs, core):
    width = received.shape[-1]
    pieces = 4
    held = PARTS // pieces
    total = NB * EA
    tall = 256

    def body(pairs_ref, core_ref, fac, src, give, keep, kept, arrived, halves, prod, out, sems):
        loads = [
            pltpu.make_async_copy(
                src.at[pl.ds(p * held, held)], arrived.at[pl.ds(p * held, held)], sems.at[p]
            )
            for p in range(pieces)
        ]
        for load in loads:
            load.start()
        prod[:, total:] = jnp.zeros((total, BS), jnp.float32)

        def convert(i, carry):
            value = arrived[pl.ds(i * OWNERS, OWNERS)].reshape(EA, width) * fac[pl.ds(i, 1), :]
            rows = pl.ds(pl.multiple_of(i * EA, EA), EA)
            halves[0, rows, :], halves[1, rows, :] = split(value)
            return carry

        ready = 0
        for g in range(total // tall):
            while ready * held * EARLY < (g + 1) * tall:
                loads[ready].wait()
                lax.fori_loop(ready * held // OWNERS, (ready + 1) * held // OWNERS, convert, 0)
                ready += 1
            cols = slice(g * tall, (g + 1) * tall)

            def row(a, carry, cols=cols):
                rows = pl.ds(pl.multiple_of(a * tall, tall), tall)
                ah, al = halves[0, rows, :], halves[1, rows, :]
                bh, bl = halves[0, cols, :], halves[1, cols, :]
                prod[rows, cols] = dot(ah, bh) + (dot(ah, bl) + dot(al, bh))
                return carry

            lax.fori_loop(0, g + 1, row, 0)
            if g:
                rows, cols = slice(g * tall, g * tall + 64), slice(g * tall - BS, g * tall)
                ah, al = halves[0, rows, :], halves[1, rows, :]
                bh, bl = halves[0, cols, :], halves[1, cols, :]
                prod[rows, cols] = dot(ah, bh) + (dot(ah, bl) + dot(al, bh))

        save = pltpu.make_async_copy(halves, kept, sems.at[pieces])
        save.start()
        lane = lax.broadcasted_iota(jnp.int32, (EARLY, BS), 1)
        sends = []

        for n, (dst, who) in enumerate(((give, 1 - core_ref[0]), (keep, core_ref[0]))):

            def store(y, at, i, j, n=n):
                rows = pl.multiple_of(i * EA, EA)
                block = j * EA // BS
                skip = j * EA - block * BS
                back = lax.rem(BS - skip, BS)
                near = pl.ds(pl.multiple_of(block * BS, BS), BS)
                far = pl.ds(pl.multiple_of(block * BS + BS, BS), BS)
                for x in range(NX):
                    which = pl.ds(rows + x * EARLY, EARLY)
                    low = pltpu.roll(prod[which, near], back, 1)
                    high = pltpu.roll(prod[which, far], back, 1)
                    out[n, x, y, at] = jnp.where(lane < BS - skip, low, high)

            each_pair(pairs_ref, who, store)
            send = pltpu.make_async_copy(out.at[n], dst, sems.at[pieces + 1 + n])
            send.start()
            sends.append(send)
        for send in sends:
            send.wait()
        save.wait()

    shape = (NX, NY, NZ * 2, EARLY, BS)
    return pl.pallas_call(
        body,
        grid_spec=pltpu.PrefetchScalarGridSpec(
            num_scalar_prefetch=2,
            grid=(1,),
            in_specs=[pl.BlockSpec(factors.shape, lambda i, *_: (0, 0)), ANYWHERE],
            out_specs=[ANYWHERE] * 3,
            scratch_shapes=[
                pltpu.VMEM(received.shape, jnp.float32),
                pltpu.VMEM((2, total, width), jnp.bfloat16),
                pltpu.VMEM((total, total + BS), jnp.float32),
                pltpu.VMEM((2,) + shape, jnp.float32),
                pltpu.SemaphoreType.DMA((pieces + 3,)),
            ],
        ),
        out_shape=[jax.ShapeDtypeStruct(shape, jnp.float32)] * 2
        + [jax.ShapeDtypeStruct((2, total, width), jnp.bfloat16)],
        compiler_params=PARAMS,
        cost_estimate=pl.CostEstimate(flops=10**11, bytes_accessed=18 * 2**20, transcendentals=0),
        name="early_tiles",
    )(pairs, core, factors, received)


def late_tiles(received, kept, factors, pairs, core, *waited):
    width = received.shape[-1]

    def body(pairs_ref, core_ref, src, fac, kept_ref, *refs):
        refs = refs[len(waited):]
        keep, gives = refs[0], refs[1:1 + NX]
        halves, late, prod, out, sems = refs[1 + NX:]
        loads = [
            pltpu.make_async_copy(
                kept_ref.at[:, pl.ds(2 * g, 2)], halves.at[:, pl.ds(2 * g, 2), pl.ds(0, EA), :], sems.at[g]
            )
            for g in range(NB // 2)
        ]
        for load in loads:
            load.start()

        def convert(i, carry):
            value = src[pl.ds(i * OWNERS, OWNERS)].reshape(LA, width) * fac[pl.ds(i, 1), :]
            rows = pl.ds(pl.multiple_of(i * LA, LA), LA)
            for part, half in enumerate(split(value)):
                halves[part, i, EA:BS, :] = half
                late[part, rows, :] = half
            return carry

        lax.fori_loop(0, NB, convert, 0)

        def column(g, carry):
            for h in range(NB // 2):

                @pl.when(g == h)
                def _(h=h):
                    loads[h].wait()

            bh, bl = (halves[part, pl.ds(2 * g, 2)].reshape(2 * BS, width) for part in (0, 1))
            ah, al = late[0], late[1]
            cols = pl.ds(pl.multiple_of(g * 256, 256), 256)
            prod[:, cols] = dot(ah, bh) + (dot(ah, bl) + dot(al, bh))
            return carry

        lax.fori_loop(0, NB // 2, column, 0)
        lane = lax.broadcasted_iota(jnp.int32, (LATE, BS), 1)
        masks = {far: (lane // (far * EARLY)) % 2 == 0 for far in (2, 1)}

        sends = []

        for n, who in enumerate((1 - core_ref[0], core_ref[0])):

            def store(y, at, i, j, n=n):
                part = prod[pl.ds(pl.multiple_of(i * LA, LA), LA), pl.ds(pl.multiple_of(j * BS, BS), BS)]
                flip = prod[pl.ds(pl.multiple_of(j * LA, LA), LA), pl.ds(pl.multiple_of(i * BS, BS), BS)]
                turn = [flip[q * LATE:(q + 1) * LATE] for q in range(OWNERS)]
                for far in (2, 1):
                    by = far * EARLY
                    for q in range(OWNERS):
                        if q & far == 0:
                            u, v = turn[q], turn[q | far]
                            turn[q] = jnp.where(masks[far], u, pltpu.roll(v, by, 1))
                            turn[q | far] = jnp.where(masks[far], pltpu.roll(u, BS - by, 1), v)
                for x in range(NX):
                    out[n, x, y, at, 0:LATE] = part[x * LATE:(x + 1) * LATE]
                    out[n, x, y, at, LATE:2 * LATE] = turn[x]

            each_pair(pairs_ref, who, store)
            for x in range(NX):
                dst = keep.at[x] if n else gives[x]
                sends.append(pltpu.make_async_copy(out.at[n, x], dst, sems.at[NB // 2 + n * NX + x]))
                sends[-1].start()
        for send in sends:
            send.wait()

    shape = (NX, NY, NZ * 2, 2 * LATE, BS)
    whole = lambda shape: pl.BlockSpec(shape, lambda i, *_: (0,) * len(shape))
    return pl.pallas_call(
        body,
        grid_spec=pltpu.PrefetchScalarGridSpec(
            num_scalar_prefetch=2,
            grid=(1,),
            in_specs=[whole(received.shape), whole(factors.shape)] + [ANYWHERE] * (1 + len(waited)),
            out_specs=[ANYWHERE] * (1 + NX),
            scratch_shapes=[
                pltpu.VMEM((2, NB, BS, width), jnp.bfloat16),
                pltpu.VMEM((2, NB * LA, width), jnp.bfloat16),
                pltpu.VMEM((NB * LA, NB * BS), jnp.float32),
                pltpu.VMEM((2,) + shape, jnp.float32),
                pltpu.SemaphoreType.DMA((NB // 2 + 2 * NX,)),
            ],
        ),
        out_shape=[jax.ShapeDtypeStruct(shape, jnp.float32)]
        + [jax.ShapeDtypeStruct(shape[1:], jnp.float32)] * NX,
        compiler_params=PARAMS,
        cost_estimate=pl.CostEstimate(flops=10**11, bytes_accessed=12 * 2**20, transcendentals=0),
        name="late_tiles",
    )(pairs, core, received, factors, kept, *waited)


def swap_cores(value):
    return lax.ppermute(value, "c", [(0, 1), (1, 0)])


def total(axis, wholes, pieces, *waited):
    size = wholes[0].shape[0]
    shape = wholes[0].shape[1:]
    place = lax.axis_index(axis).astype(jnp.int32).reshape(1)

    def body(place_ref, *refs):
        whole_refs = refs[:len(wholes)]
        piece_refs = refs[len(wholes):len(wholes) + len(pieces)]
        outs = refs[len(refs) - size:]
        for d in range(size):
            at = lax.rem(place_ref[0] + d, size)
            for s in range(size):

                @pl.when(at == s)
                def _(d=d, s=s):
                    value = whole_refs[0][s]
                    for ref in whole_refs[1:]:
                        value = value + ref[s]
                    if pieces:
                        value = value + piece_refs[s][...]
                    outs[d][...] = value

    full = lambda shape: pl.BlockSpec(shape, lambda i, *_: (0,) * len(shape))
    return pl.pallas_call(
        body,
        grid_spec=pltpu.PrefetchScalarGridSpec(
            num_scalar_prefetch=1,
            grid=(1,),
            in_specs=[full(wholes[0].shape)] * len(wholes)
            + [full(shape)] * len(pieces)
            + [ANYWHERE] * len(waited),
            out_specs=[full(shape)] * size,
        ),
        out_shape=[jax.ShapeDtypeStruct(shape, jnp.float32)] * size,
        compiler_params=PARAMS,
        cost_estimate=SMALL,
        name="total",
    )(place, *wholes, *pieces, *waited)


def send_on(axis, parts):
    size = len(parts)
    return [parts[0]] + [
        lax.ppermute(parts[d], axis, [(s, (s + d) % size) for s in range(size)]) for d in range(1, size)
    ]


def join(early, late):
    def body(*refs):
        out = refs[-1]
        for srcs, low, high in ((refs[:NY], 0, EARLY), (refs[NY:-1], EARLY, EARLY + 2 * LATE)):
            value = srcs[0][...]
            for src in srcs[1:]:
                value = value + src[...]
            out[:, low:high] = value

    return pl.pallas_call(
        body,
        out_shape=jax.ShapeDtypeStruct((NZ * 2, EARLY + 2 * LATE, BS), jnp.float32),
        compiler_params=PARAMS,
        cost_estimate=SMALL,
        name="join",
    )(*early, *late)


def finish(parts, scale):
    count = parts.shape[1]

    def body(src, out):
        lane = lax.broadcasted_iota(jnp.int32, (OWNERS * LATE, BS), 1)
        for w in range(count):
            value = src[0, w]
            for s in range(1, NZ):
                value = value + src[s, w]
            value = value * scale
            packed = value[EARLY + LATE:]
            stacked = jnp.concatenate(
                [packed if q == 0 else pltpu.roll(packed, BS - q * EARLY, 1) for q in range(OWNERS)], axis=0
            )
            turned = jnp.concatenate([stacked] * (BS // (OWNERS * LATE)), axis=0).T
            rows = jnp.concatenate(
                [
                    jnp.where(lane[:EARLY] < EA, value[:EARLY], turned[:EARLY]),
                    value[EARLY:EARLY + LATE],
                ],
                axis=0,
            )
            result = jnp.zeros((EARLY + LATE, BS), jnp.float32)
            for o in range(OWNERS):
                at = o * (EARLY + LATE)
                for low, size, source in ((at, EARLY, o * EARLY), (at + EARLY, LATE, EA + o * LATE)):
                    by = (low - source) % BS
                    moved = pltpu.roll(rows, by, 1) if by else rows
                    result = jnp.where((lane >= low) & (lane < low + size), moved, result)
            out[w] = result

    return pl.pallas_call(
        body,
        out_shape=jax.ShapeDtypeStruct((count, EARLY + LATE, BS), jnp.float32),
        compiler_params=PARAMS,
        cost_estimate=SMALL,
        name="finish",
    )(parts)


def on_device(jac, obs_group, group_weight, pattern, pairs):
    total_obs = jac.shape[1] * NX
    core = lax.axis_index("c").astype(jnp.int32).reshape(1)
    listed = pairs.reshape(-1)
    choice = obs_group[0][None, :] == jnp.arange(group_weight.shape[0], dtype=jnp.int32)[:, None]
    root = jnp.sum(jnp.where(choice, group_weight[:, None], 0.0), axis=0)
    factors = pattern[0, 0].astype(jnp.float32)[:, None] * root[None, :]

    early = lax.all_to_all(relayout(jac, 0, EARLY), OBS_AXES, 0, 0, tiled=True)
    late = lax.all_to_all(relayout(jac, EARLY, LATE), OBS_AXES, 0, 0, tiled=True)

    give, keep, kept = early_tiles(early, factors, listed, core)
    kept = kept.reshape(2, NB, EA, -1)
    parts = total("x", [keep, swap_cores(give)], [])
    keep, *gives = late_tiles(late, kept, factors, listed, core, *parts)
    parts = total("y", send_on("x", parts), [])
    rest = total("x", [keep], [swap_cores(give) for give in gives], *parts)
    parts = send_on("y", parts)
    rest = total("y", send_on("x", rest), [])
    rest = send_on("y", rest)
    message = join(parts, rest).reshape(NZ, 2, EARLY + 2 * LATE, BS)
    owned = lax.all_to_all(message, "z", 0, 0, tiled=True)
    return finish(owned, 1.0 / math.sqrt(total_obs))


def solution(mesh):
    fine = Mesh(mesh.devices.reshape(NZ, NY, NC, NX), ("z", "y", "c", "x"))
    return jax.shard_map(
        on_device,
        mesh=fine,
        in_specs=(P(OBS_AXES, "x"), P("x", OBS_AXES), P(), P("x", OBS_AXES, None), P()),
        out_specs=P(OBS_AXES, "x", None),
        check_vma=False,
    )
```

```python
import math

import jax
import jax.numpy as jnp
from jax import lax
from jax.experimental import pallas as pl
from jax.experimental.pallas import tpu as pltpu
from jax.sharding import Mesh, PartitionSpec as P

NZ, NY, NC, NX = 8, 4, 2, 4
PARTS = NZ * NY * NC
OBS_AXES = ("z", "y", "c")
NB, BS = 16, 128
OWNERS = 4
EARLY, LATE = 24, 8
EA, LA = OWNERS * EARLY, OWNERS * LATE
PACKED = 2 * EARLY - 8
VMEM_LIMIT = 60 * 1024 * 1024
SMALL = pl.CostEstimate(flops=1, bytes_accessed=1, transcendentals=0)
PARAMS = pltpu.CompilerParams(vmem_limit_bytes=VMEM_LIMIT)
ANYWHERE = pl.BlockSpec(memory_space=pl.ANY)


def relayout(jac, start, rows):
    width = jac.shape[1] // PARTS

    def body(src, out, hold, sems):
        loads, stores = [], []
        for i in range(PARTS):
            part = src.at[pl.ds(start, rows), pl.ds(i * width, width)]
            loads.append(pltpu.make_async_copy(part, hold.at[i], sems.at[0, i]))
            stores.append(pltpu.make_async_copy(hold.at[i], out.at[i], sems.at[1, i]))
        for load in loads:
            load.start()
        for load, store in zip(loads, stores):
            load.wait()
            store.start()
        for store in stores:
            store.wait()

    shape = (PARTS, rows, width)
    return pl.pallas_call(
        body,
        in_specs=[ANYWHERE],
        out_specs=ANYWHERE,
        out_shape=jax.ShapeDtypeStruct(shape, jac.dtype),
        scratch_shapes=[pltpu.VMEM(shape, jac.dtype), pltpu.SemaphoreType.DMA((2, PARTS))],
        compiler_params=PARAMS,
        cost_estimate=SMALL,
        name="relayout",
    )(jac)


def dot(u, v):
    return lax.dot_general(u, v, (((1,), (1,)), ((), ())), preferred_element_type=jnp.float32)


def split(value):
    top = value.astype(jnp.bfloat16)
    return top, (value - top.astype(jnp.float32)).astype(jnp.bfloat16)


def each_owner(pairs_ref, mine, store):
    def one(s, carry):
        z, y = s // NY, s % NY
        k = ((z * NY + y) * NC + mine) * 2
        store(z, y, [(pairs_ref[2 * k + 2 * w], pairs_ref[2 * k + 2 * w + 1]) for w in range(2)])
        return carry

    lax.fori_loop(0, NZ * NY, one, 0, unroll=4)


def early_tiles(received, factors, pairs, core):
    width = received.shape[-1]
    pieces = 4
    held = PARTS // pieces
    total = NB * EA
    tall = 256

    def body(pairs_ref, core_ref, fac, src, give, keep, kept, arrived, halves, prod, out, sems):
        loads = [
            pltpu.make_async_copy(
                src.at[pl.ds(p * held, held)], arrived.at[pl.ds(p * held, held)], sems.at[p]
            )
            for p in range(pieces)
        ]
        for load in loads:
            load.start()
        prod[:, total:] = jnp.zeros((total, BS), jnp.float32)

        def convert(i, carry):
            value = arrived[pl.ds(i * OWNERS, OWNERS)].reshape(EA, width) * fac[pl.ds(i, 1), :]
            rows = pl.ds(pl.multiple_of(i * EA, EA), EA)
            halves[0, rows, :], halves[1, rows, :] = split(value)
            return carry

        ready = 0
        for g in range(total // tall):
            while ready * held * EARLY < (g + 1) * tall:
                loads[ready].wait()
                lax.fori_loop(ready * held // OWNERS, (ready + 1) * held // OWNERS, convert, 0)
                ready += 1
            cols = slice(g * tall, (g + 1) * tall)

            def row(a, carry, cols=cols):
                rows = pl.ds(pl.multiple_of(a * tall, tall), tall)
                ah, al = halves[0, rows, :], halves[1, rows, :]
                bh, bl = halves[0, cols, :], halves[1, cols, :]
                prod[rows, cols] = dot(ah, bh) + (dot(ah, bl) + dot(al, bh))
                return carry

            lax.fori_loop(0, g + 1, row, 0)
            if g:
                rows, cols = slice(g * tall, g * tall + 64), slice(g * tall - BS, g * tall)
                ah, al = halves[0, rows, :], halves[1, rows, :]
                bh, bl = halves[0, cols, :], halves[1, cols, :]
                prod[rows, cols] = dot(ah, bh) + (dot(ah, bl) + dot(al, bh))

        save = pltpu.make_async_copy(halves, kept, sems.at[pieces])
        save.start()
        lane = lax.broadcasted_iota(jnp.int32, (EARLY, BS), 1)
        sends = []

        for n, (dst, who) in enumerate(((give, 1 - core_ref[0]), (keep, core_ref[0]))):

            def store(z, y, pairs, n=n):
                tiles = []
                for i, j in pairs:
                    rows = pl.multiple_of(i * EA, EA)
                    block = j * EA // BS
                    skip = j * EA - block * BS
                    back = lax.rem(BS - skip, BS)
                    near = pl.ds(pl.multiple_of(block * BS, BS), BS)
                    far = pl.ds(pl.multiple_of(block * BS + BS, BS), BS)
                    tiles.append([])
                    for x in range(NX):
                        which = pl.ds(rows + x * EARLY, EARLY)
                        low = pltpu.roll(prod[which, near], back, 1)
                        high = pltpu.roll(prod[which, far], back, 1)
                        tiles[-1].append(jnp.where(lane < BS - skip, low, high))
                for x in range(NX):
                    head, tail = tiles[0][x], tiles[1][x]
                    last = tail[EARLY - 8:]
                    gaps = [pltpu.roll(last, EA - LA * q, 1) for q in range(EARLY // 8)]
                    out[n, x, y, z, 0:EARLY] = jnp.where(lane < EA, head, jnp.concatenate(gaps, axis=0))
                    out[n, x, y, z, EARLY:PACKED] = tail[:EARLY - 8]

            each_owner(pairs_ref, who, store)
            send = pltpu.make_async_copy(out.at[n], dst, sems.at[pieces + 1 + n])
            send.start()
            sends.append(send)
        for send in sends:
            send.wait()
        save.wait()

    shape = (NX, NY, NZ, PACKED, BS)
    return pl.pallas_call(
        body,
        grid_spec=pltpu.PrefetchScalarGridSpec(
            num_scalar_prefetch=2,
            grid=(1,),
            in_specs=[pl.BlockSpec(factors.shape, lambda i, *_: (0, 0)), ANYWHERE],
            out_specs=[ANYWHERE] * 3,
            scratch_shapes=[
                pltpu.VMEM(received.shape, jnp.float32),
                pltpu.VMEM((2, total, width), jnp.bfloat16),
                pltpu.VMEM((total, total + BS), jnp.float32),
                pltpu.VMEM((2,) + shape, jnp.float32),
                pltpu.SemaphoreType.DMA((pieces + 3,)),
            ],
        ),
        out_shape=[jax.ShapeDtypeStruct(shape, jnp.float32)] * 2
        + [jax.ShapeDtypeStruct((2, total, width), jnp.bfloat16)],
        compiler_params=PARAMS,
        cost_estimate=pl.CostEstimate(flops=10**11, bytes_accessed=18 * 2**20, transcendentals=0),
        name="early_tiles",
    )(pairs, core, factors, received)


def late_tiles(received, kept, factors, pairs, core, *waited):
    width = received.shape[-1]

    def body(pairs_ref, core_ref, src, fac, kept_ref, *refs):
        refs = refs[len(waited):]
        keep, gives = refs[0], refs[1:1 + NX]
        halves, late, prod, out, sems = refs[1 + NX:]
        loads = [
            pltpu.make_async_copy(
                kept_ref.at[:, pl.ds(2 * g, 2)], halves.at[:, pl.ds(2 * g, 2), pl.ds(0, EA), :], sems.at[g]
            )
            for g in range(NB // 2)
        ]
        for load in loads:
            load.start()

        def convert(i, carry):
            value = src[pl.ds(i * OWNERS, OWNERS)].reshape(LA, width) * fac[pl.ds(i, 1), :]
            rows = pl.ds(pl.multiple_of(i * LA, LA), LA)
            for part, half in enumerate(split(value)):
                halves[part, i, EA:BS, :] = half
                late[part, rows, :] = half
            return carry

        lax.fori_loop(0, NB, convert, 0)

        def column(g, carry):
            for h in range(NB // 2):

                @pl.when(g == h)
                def _(h=h):
                    loads[h].wait()

            bh, bl = (halves[part, pl.ds(2 * g, 2)].reshape(2 * BS, width) for part in (0, 1))
            ah, al = late[0], late[1]
            cols = pl.ds(pl.multiple_of(g * 256, 256), 256)
            prod[:, cols] = dot(ah, bh) + (dot(ah, bl) + dot(al, bh))
            return carry

        lax.fori_loop(0, NB // 2, column, 0)
        lane = lax.broadcasted_iota(jnp.int32, (LATE, BS), 1)
        masks = {far: (lane // (far * EARLY)) % 2 == 0 for far in (2, 1)}

        sends = []

        for n, who in enumerate((1 - core_ref[0], core_ref[0])):

            def store(z, y, pairs, n=n):
                for w, (i, j) in enumerate(pairs):
                    part = prod[pl.ds(pl.multiple_of(i * LA, LA), LA), pl.ds(pl.multiple_of(j * BS, BS), BS)]
                    flip = prod[pl.ds(pl.multiple_of(j * LA, LA), LA), pl.ds(pl.multiple_of(i * BS, BS), BS)]
                    turn = [flip[q * LATE:(q + 1) * LATE] for q in range(OWNERS)]
                    for far in (2, 1):
                        by = far * EARLY
                        for q in range(OWNERS):
                            if q & far == 0:
                                u, v = turn[q], turn[q | far]
                                turn[q] = jnp.where(masks[far], u, pltpu.roll(v, by, 1))
                                turn[q | far] = jnp.where(masks[far], pltpu.roll(u, BS - by, 1), v)
                    for x in range(NX):
                        out[n, x, z, y, w, 0:LATE] = part[x * LATE:(x + 1) * LATE]
                        out[n, x, z, y, w, LATE:2 * LATE] = turn[x]

            each_owner(pairs_ref, who, store)
            for x in range(NX):
                dst = keep.at[x] if n else gives[x]
                sends.append(pltpu.make_async_copy(out.at[n, x], dst, sems.at[NB // 2 + n * NX + x]))
                sends[-1].start()
        for send in sends:
            send.wait()

    shape = (NX, NZ, NY, 2, 2 * LATE, BS)
    whole = lambda shape: pl.BlockSpec(shape, lambda i, *_: (0,) * len(shape))
    return pl.pallas_call(
        body,
        grid_spec=pltpu.PrefetchScalarGridSpec(
            num_scalar_prefetch=2,
            grid=(1,),
            in_specs=[whole(received.shape), whole(factors.shape)] + [ANYWHERE] * (1 + len(waited)),
            out_specs=[ANYWHERE] * (1 + NX),
            scratch_shapes=[
                pltpu.VMEM((2, NB, BS, width), jnp.bfloat16),
                pltpu.VMEM((2, NB * LA, width), jnp.bfloat16),
                pltpu.VMEM((NB * LA, NB * BS), jnp.float32),
                pltpu.VMEM((2,) + shape, jnp.float32),
                pltpu.SemaphoreType.DMA((NB // 2 + 2 * NX,)),
            ],
        ),
        out_shape=[jax.ShapeDtypeStruct(shape, jnp.float32)]
        + [jax.ShapeDtypeStruct(shape[1:], jnp.float32)] * NX,
        compiler_params=PARAMS,
        cost_estimate=pl.CostEstimate(flops=10**11, bytes_accessed=12 * 2**20, transcendentals=0),
        name="late_tiles",
    )(pairs, core, received, factors, kept, *waited)


def swap_cores(value):
    return lax.ppermute(value, "c", [(0, 1), (1, 0)])


def total(axis, wholes, pieces, *waited):
    size = wholes[0].shape[0]
    shape = wholes[0].shape[1:]
    place = lax.axis_index(axis).astype(jnp.int32).reshape(1)

    def body(place_ref, *refs):
        whole_refs = refs[:len(wholes)]
        piece_refs = refs[len(wholes):len(wholes) + len(pieces)]
        outs = refs[len(refs) - size:]
        for d in range(size):
            at = lax.rem(place_ref[0] + d, size)
            for s in range(size):

                @pl.when(at == s)
                def _(d=d, s=s):
                    value = whole_refs[0][s]
                    for ref in whole_refs[1:]:
                        value = value + ref[s]
                    if pieces:
                        value = value + piece_refs[s][...]
                    outs[d][...] = value

    tail = (0,) * (len(shape) - 1)
    cut = (shape[0] // 2,) + shape[1:]
    full = pl.BlockSpec((size,) + cut, lambda i, *_: (0, i) + tail)
    part = pl.BlockSpec(cut, lambda i, *_: (i,) + tail)
    return pl.pallas_call(
        body,
        grid_spec=pltpu.PrefetchScalarGridSpec(
            num_scalar_prefetch=1,
            grid=(2,),
            in_specs=[full] * len(wholes) + [part] * len(pieces) + [ANYWHERE] * len(waited),
            out_specs=[part] * size,
        ),
        out_shape=[jax.ShapeDtypeStruct(shape, jnp.float32)] * size,
        compiler_params=PARAMS,
        cost_estimate=SMALL,
        name="total",
    )(place, *wholes, *pieces, *waited)


def send_on(axis, parts):
    size = len(parts)
    return [parts[0]] + [
        lax.ppermute(parts[d], axis, [(s, (s + d) % size) for s in range(size)]) for d in range(1, size)
    ]


def merge(terms, *waited):
    def body(*refs):
        value = refs[0][...]
        for ref in refs[1:len(terms)]:
            value = value + ref[...]
        refs[-1][...] = value

    vmem = pl.BlockSpec(memory_space=pltpu.VMEM)
    return pl.pallas_call(
        body,
        in_specs=[vmem] * len(terms) + [ANYWHERE] * len(waited),
        out_specs=vmem,
        out_shape=jax.ShapeDtypeStruct(terms[0].shape, jnp.float32),
        compiler_params=PARAMS,
        cost_estimate=SMALL,
        name="merge",
    )(*terms, *waited)


def finish(early, late, scale):
    count = late.shape[1]

    def body(first, second, out):
        lane = lax.broadcasted_iota(jnp.int32, (OWNERS * LATE, BS), 1)
        head = sum((first[s] for s in range(1, first.shape[0])), first[0]) * scale
        for w in range(count):
            rest = sum((second[s, w] for s in range(1, second.shape[0])), second[0, w]) * scale
            if w == 0:
                top = head[:EARLY]
            else:
                last = jnp.zeros((8, BS), jnp.float32)
                for q in range(EARLY // 8):
                    moved = pltpu.roll(head[8 * q:8 * q + 8], (LA * q - EA) % BS, 1)
                    last = jnp.where(lane[:8] // LA == q, moved, last)
                top = jnp.concatenate([head[EARLY:], last], axis=0)
            packed = rest[LATE:]
            stacked = jnp.concatenate(
                [packed if q == 0 else pltpu.roll(packed, BS - q * EARLY, 1) for q in range(OWNERS)], axis=0
            )
            turned = jnp.concatenate([stacked] * (BS // (OWNERS * LATE)), axis=0).T
            rows = jnp.concatenate(
                [
                    jnp.where(lane[:EARLY] < EA, top, turned[:EARLY]),
                    rest[:LATE],
                ],
                axis=0,
            )
            result = jnp.zeros((EARLY + LATE, BS), jnp.float32)
            for o in range(OWNERS):
                at = o * (EARLY + LATE)
                for low, size, source in ((at, EARLY, o * EARLY), (at + EARLY, LATE, EA + o * LATE)):
                    by = (low - source) % BS
                    moved = pltpu.roll(rows, by, 1) if by else rows
                    result = jnp.where((lane >= low) & (lane < low + size), moved, result)
            out[w] = result

    return pl.pallas_call(
        body,
        out_shape=jax.ShapeDtypeStruct((count, EARLY + LATE, BS), jnp.float32),
        compiler_params=PARAMS,
        cost_estimate=SMALL,
        name="finish",
    )(early, late)


def on_device(jac, obs_group, group_weight, pattern, pairs):
    total_obs = jac.shape[1] * NX
    core = lax.axis_index("c").astype(jnp.int32).reshape(1)
    listed = pairs.reshape(-1)
    choice = obs_group[0][None, :] == jnp.arange(group_weight.shape[0], dtype=jnp.int32)[:, None]
    root = jnp.sum(jnp.where(choice, group_weight[:, None], 0.0), axis=0)
    factors = pattern[0, 0].astype(jnp.float32)[:, None] * root[None, :]

    early = lax.all_to_all(relayout(jac, 0, EARLY), OBS_AXES, 0, 0, tiled=True)
    late = lax.all_to_all(relayout(jac, EARLY, LATE), OBS_AXES, 0, 0, tiled=True)

    give, keep, kept = early_tiles(early, factors, listed, core)
    kept = kept.reshape(2, NB, EA, -1)
    parts = total("x", [keep, swap_cores(give)], [])
    keep, *gives = late_tiles(late, kept, factors, listed, core, *parts)
    parts = total("y", send_on("x", parts), [])
    rest = total("x", [keep], [swap_cores(give) for give in gives], *parts)
    parts = merge(send_on("y", parts))
    parts = lax.all_to_all(parts, "z", 0, 0, tiled=True)
    rest = merge(send_on("x", rest), parts).reshape(NZ * NY, 2, 2 * LATE, BS)
    rest = lax.all_to_all(rest, ("z", "y"), 0, 0, tiled=True)
    return finish(parts, rest, 1.0 / math.sqrt(total_obs))


def solution(mesh):
    fine = Mesh(mesh.devices.reshape(NZ, NY, NC, NX), ("z", "y", "c", "x"))
    return jax.shard_map(
        on_device,
        mesh=fine,
        in_specs=(P(OBS_AXES, "x"), P("x", OBS_AXES), P(), P("x", OBS_AXES, None), P()),
        out_specs=P(OBS_AXES, "x", None),
        check_vma=False,
    )
```

```python
import math

import jax
import jax.numpy as jnp
from jax import lax
from jax.experimental import pallas as pl
from jax.experimental.pallas import tpu as pltpu
from jax.sharding import Mesh, PartitionSpec as P

NZ, NY, NC, NX = 8, 4, 2, 4
PARTS = NZ * NY * NC
OBS_AXES = ("z", "y", "c")
NB, BS = 16, 128
OWNERS = 4
EARLY, LATE = 24, 8
EA, LA = OWNERS * EARLY, OWNERS * LATE
PACKED = 2 * EARLY - 8
ANYWHERE = pl.BlockSpec(memory_space=pl.ANY)
SMALL = pl.CostEstimate(flops=1, bytes_accessed=1, transcendentals=0)


def room(mebibytes):
    return pltpu.CompilerParams(vmem_limit_bytes=mebibytes * 2**20)


def relayout(jac, start, rows):
    width = jac.shape[1] // PARTS

    loads = 8
    span = PARTS // loads

    def body(src, out, hold, sems):
        copies = []
        for n in range(loads):
            lanes = pl.ds(n * span * width, span * width)
            copies.append(pltpu.make_async_copy(src.at[pl.ds(start, rows), lanes], hold.at[:, lanes], sems.at[n]))
            copies[-1].start()
        stores = []
        for n in range(loads):
            copies[n].wait()
            for i in range(n * span, (n + 1) * span):
                lanes = pl.ds(i * width, width)
                stores.append(pltpu.make_async_copy(hold.at[:, lanes], out.at[i], sems.at[loads + i]))
                stores[-1].start()
        for store in stores:
            store.wait()

    return pl.pallas_call(
        body,
        in_specs=[ANYWHERE],
        out_specs=ANYWHERE,
        out_shape=jax.ShapeDtypeStruct((PARTS, rows, width), jac.dtype),
        scratch_shapes=[
            pltpu.VMEM((rows, PARTS * width), jac.dtype),
            pltpu.SemaphoreType.DMA((loads + PARTS,)),
        ],
        compiler_params=room(60),
        cost_estimate=SMALL,
        name="relayout",
    )(jac)


def dot(u, v):
    return lax.dot_general(u, v, (((1,), (1,)), ((), ())), preferred_element_type=jnp.float32)


def split(value):
    top = value.astype(jnp.bfloat16)
    return top, (value - top.astype(jnp.float32)).astype(jnp.bfloat16)


def each_owner(pairs_ref, mine, store):
    def one(s, carry):
        z, y = s // NY, s % NY
        k = ((z * NY + y) * NC + mine) * 2
        store(z, y, [(pairs_ref[2 * k + 2 * w], pairs_ref[2 * k + 2 * w + 1]) for w in range(2)])
        return carry

    lax.fori_loop(0, NZ * NY, one, 0, unroll=4)


def early_tiles(received, factors, pairs, core):
    width = received.shape[-1]
    pieces = 4
    held = PARTS // pieces
    total = NB * EA
    tall = 256

    def body(pairs_ref, core_ref, fac, src, give, keep, kept, arrived, halves, prod, out, sems):
        loads = [
            pltpu.make_async_copy(
                src.at[pl.ds(p * held, held)], arrived.at[pl.ds(p * held, held)], sems.at[p]
            )
            for p in range(pieces)
        ]
        for load in loads:
            load.start()
        lane = lax.broadcasted_iota(jnp.int32, (tall, BS), 1)

        def convert(i, carry):
            value = arrived[pl.ds(i * OWNERS, OWNERS)].reshape(EA, width) * fac[pl.ds(i, 1), :]
            rows = pl.ds(pl.multiple_of(i * EA, EA), EA)
            halves[0, rows, :], halves[1, rows, :] = split(value)
            return carry

        def place(rows, start, value):
            stop = start + value.shape[1]
            for j in range(start // EA, -(-stop // EA)):
                low, high = max(j * EA, start), min((j + 1) * EA, stop)
                by = (start - j * EA) % BS
                moved = None
                for t in range((low - start) // BS, (high - start - 1) // BS + 1):
                    part = value[:, t * BS:(t + 1) * BS]
                    part = pltpu.roll(part, by, 1) if by else part
                    moved = part if moved is None else jnp.where(lane < start + t * BS - j * EA, moved, part)
                block = slice(j * BS, (j + 1) * BS)
                if low > j * EA:
                    moved = jnp.where(lane < low - j * EA, prod[rows, block], moved)
                prod[rows, block] = moved

        ready = 0
        for g in range(total // tall):
            while ready * held * EARLY < (g + 1) * tall:
                loads[ready].wait()
                lax.fori_loop(ready * held // OWNERS, (ready + 1) * held // OWNERS, convert, 0)
                ready += 1
            cols = slice(g * tall, (g + 1) * tall)

            def row(a, carry, cols=cols, g=g):
                rows = pl.ds(pl.multiple_of(a * tall, tall), tall)
                ah, al = halves[0, rows, :], halves[1, rows, :]
                bh, bl = halves[0, cols, :], halves[1, cols, :]
                place(rows, g * tall, dot(ah, bh) + (dot(ah, bl) + dot(al, bh)))
                return carry

            lax.fori_loop(0, g + 1, row, 0)
            if g * tall % EA:
                rows = slice(g * tall, g * tall + 64)
                cols = slice(g * tall // EA * EA, g * tall)
                ah, al = halves[0, rows, :], halves[1, rows, :]
                bh, bl = halves[0, cols, :], halves[1, cols, :]
                value = dot(ah, bh) + (dot(ah, bl) + dot(al, bh))
                at = g * tall // EA * BS
                prod[rows, at:at + value.shape[1]] = value

        save = pltpu.make_async_copy(halves, kept, sems.at[pieces])
        save.start()
        sends = []

        for n, (dst, who) in enumerate(((give, 1 - core_ref[0]), (keep, core_ref[0]))):

            def store(z, y, pairs, n=n):
                tiles = []
                for i, j in pairs:
                    rows = pl.multiple_of(i * EA, EA)
                    cols = pl.ds(pl.multiple_of(j * BS, BS), BS)
                    tiles.append([prod[pl.ds(rows + x * EARLY, EARLY), cols] for x in range(NX)])
                for x in range(NX):
                    head, tail = tiles[0][x], tiles[1][x]
                    last = tail[EARLY - 8:]
                    gaps = [pltpu.roll(last, EA - LA * q, 1) for q in range(EARLY // 8)]
                    out[n, x, y, z, 0:EARLY] = jnp.where(lane[:EARLY] < EA, head, jnp.concatenate(gaps, axis=0))
                    out[n, x, y, z, EARLY:PACKED] = tail[:EARLY - 8]

            each_owner(pairs_ref, who, store)
            send = pltpu.make_async_copy(out.at[n], dst, sems.at[pieces + 1 + n])
            send.start()
            sends.append(send)
        for send in sends:
            send.wait()
        save.wait()

    shape = (NX, NY, NZ, PACKED, BS)
    return pl.pallas_call(
        body,
        grid_spec=pltpu.PrefetchScalarGridSpec(
            num_scalar_prefetch=2,
            grid=(1,),
            in_specs=[pl.BlockSpec(factors.shape, lambda i, *_: (0, 0)), ANYWHERE],
            out_specs=[ANYWHERE] * 3,
            scratch_shapes=[
                pltpu.VMEM(received.shape, jnp.float32),
                pltpu.VMEM((2, total, width), jnp.bfloat16),
                pltpu.VMEM((total, NB * BS), jnp.float32),
                pltpu.VMEM((2,) + shape, jnp.float32),
                pltpu.SemaphoreType.DMA((pieces + 3,)),
            ],
        ),
        out_shape=[jax.ShapeDtypeStruct(shape, jnp.float32)] * 2
        + [jax.ShapeDtypeStruct((2, total, width), jnp.bfloat16)],
        compiler_params=room(58),
        cost_estimate=pl.CostEstimate(flops=10**11, bytes_accessed=18 * 2**20, transcendentals=0),
        name="early_tiles",
    )(pairs, core, factors, received)


def late_tiles(received, kept, factors, pairs, core, *waited):
    width = received.shape[-1]

    def body(pairs_ref, core_ref, src, fac, kept_ref, *refs):
        refs = refs[len(waited):]
        keep, gives = refs[0], refs[1:1 + NX]
        halves, late, prod, out, sems = refs[1 + NX:]
        loads = [
            pltpu.make_async_copy(
                kept_ref.at[:, pl.ds(2 * g, 2)], halves.at[:, pl.ds(2 * g, 2), pl.ds(0, EA), :], sems.at[g]
            )
            for g in range(NB // 2)
        ]
        for load in loads:
            load.start()

        def convert(i, carry):
            value = src[pl.ds(i * OWNERS, OWNERS)].reshape(LA, width) * fac[pl.ds(i, 1), :]
            rows = pl.ds(pl.multiple_of(i * LA, LA), LA)
            for part, half in enumerate(split(value)):
                halves[part, i, EA:BS, :] = half
                late[part, rows, :] = half
            return carry

        lax.fori_loop(0, NB, convert, 0)

        def column(g, carry):
            for h in range(NB // 2):

                @pl.when(g == h)
                def _(h=h):
                    loads[h].wait()

            bh, bl = (halves[part, pl.ds(2 * g, 2)].reshape(2 * BS, width) for part in (0, 1))
            ah, al = late[0], late[1]
            cols = pl.ds(pl.multiple_of(g * 256, 256), 256)
            prod[:, cols] = dot(ah, bh) + (dot(ah, bl) + dot(al, bh))
            return carry

        lax.fori_loop(0, NB // 2, column, 0)
        lane = lax.broadcasted_iota(jnp.int32, (LATE, BS), 1)
        masks = {far: (lane // (far * EARLY)) % 2 == 0 for far in (2, 1)}

        sends = []

        for n, who in enumerate((1 - core_ref[0], core_ref[0])):

            def store(z, y, pairs, n=n):
                for w, (i, j) in enumerate(pairs):
                    part = prod[pl.ds(pl.multiple_of(i * LA, LA), LA), pl.ds(pl.multiple_of(j * BS, BS), BS)]
                    flip = prod[pl.ds(pl.multiple_of(j * LA, LA), LA), pl.ds(pl.multiple_of(i * BS, BS), BS)]
                    turn = [flip[q * LATE:(q + 1) * LATE] for q in range(OWNERS)]
                    for far in (2, 1):
                        by = far * EARLY
                        for q in range(OWNERS):
                            if q & far == 0:
                                u, v = turn[q], turn[q | far]
                                turn[q] = jnp.where(masks[far], u, pltpu.roll(v, by, 1))
                                turn[q | far] = jnp.where(masks[far], pltpu.roll(u, BS - by, 1), v)
                    for x in range(NX):
                        out[n, x, z, y, w, 0:LATE] = part[x * LATE:(x + 1) * LATE]
                        out[n, x, z, y, w, LATE:2 * LATE] = turn[x]

            each_owner(pairs_ref, who, store)
            for x in range(NX):
                dst = keep.at[x] if n else gives[x]
                sends.append(pltpu.make_async_copy(out.at[n, x], dst, sems.at[NB // 2 + n * NX + x]))
                sends[-1].start()
        for send in sends:
            send.wait()

    shape = (NX, NZ, NY, 2, 2 * LATE, BS)
    whole = lambda shape: pl.BlockSpec(shape, lambda i, *_: (0,) * len(shape))
    return pl.pallas_call(
        body,
        grid_spec=pltpu.PrefetchScalarGridSpec(
            num_scalar_prefetch=2,
            grid=(1,),
            in_specs=[whole(received.shape), whole(factors.shape)] + [ANYWHERE] * (1 + len(waited)),
            out_specs=[ANYWHERE] * (1 + NX),
            scratch_shapes=[
                pltpu.VMEM((2, NB, BS, width), jnp.bfloat16),
                pltpu.VMEM((2, NB * LA, width), jnp.bfloat16),
                pltpu.VMEM((NB * LA, NB * BS), jnp.float32),
                pltpu.VMEM((2,) + shape, jnp.float32),
                pltpu.SemaphoreType.DMA((NB // 2 + 2 * NX,)),
            ],
        ),
        out_shape=[jax.ShapeDtypeStruct(shape, jnp.float32)]
        + [jax.ShapeDtypeStruct(shape[1:], jnp.float32)] * NX,
        compiler_params=room(58),
        cost_estimate=pl.CostEstimate(flops=10**11, bytes_accessed=12 * 2**20, transcendentals=0),
        name="late_tiles",
    )(pairs, core, received, factors, kept, *waited)


def swap_cores(value):
    return lax.ppermute(value, "c", [(0, 1), (1, 0)])


def total(axis, wholes, pieces, *waited):
    size = wholes[0].shape[0]
    shape = wholes[0].shape[1:]
    place = lax.axis_index(axis).astype(jnp.int32).reshape(1)

    def body(place_ref, *refs):
        whole_refs = refs[:len(wholes)]
        piece_refs = refs[len(wholes):len(wholes) + len(pieces)]
        outs = refs[len(refs) - size:]
        for d in range(size):
            at = lax.rem(place_ref[0] + d, size)
            for s in range(size):

                @pl.when(at == s)
                def _(d=d, s=s):
                    value = whole_refs[0][s]
                    for ref in whole_refs[1:]:
                        value = value + ref[s]
                    if pieces:
                        value = value + piece_refs[s][...]
                    outs[d][...] = value

    tail = (0,) * (len(shape) - 1)
    cut = (shape[0] // 2,) + shape[1:]
    full = pl.BlockSpec((size,) + cut, lambda i, *_: (0, i) + tail)
    part = pl.BlockSpec(cut, lambda i, *_: (i,) + tail)
    return pl.pallas_call(
        body,
        grid_spec=pltpu.PrefetchScalarGridSpec(
            num_scalar_prefetch=1,
            grid=(2,),
            in_specs=[full] * len(wholes) + [part] * len(pieces) + [ANYWHERE] * len(waited),
            out_specs=[part] * size,
        ),
        out_shape=[jax.ShapeDtypeStruct(shape, jnp.float32)] * size,
        compiler_params=room(16),
        cost_estimate=SMALL,
        name="total",
    )(place, *wholes, *pieces, *waited)


def send_on(axis, parts):
    size = len(parts)
    return [parts[0]] + [
        lax.ppermute(parts[d], axis, [(s, (s + d) % size) for s in range(size)]) for d in range(1, size)
    ]


def merge(terms, *waited):
    def body(*refs):
        value = refs[0][...]
        for ref in refs[1:len(terms)]:
            value = value + ref[...]
        refs[-1][...] = value

    vmem = pl.BlockSpec(memory_space=pltpu.VMEM)
    return pl.pallas_call(
        body,
        in_specs=[vmem] * len(terms) + [ANYWHERE] * len(waited),
        out_specs=vmem,
        out_shape=jax.ShapeDtypeStruct(terms[0].shape, jnp.float32),
        compiler_params=room(16),
        cost_estimate=SMALL,
        name="merge",
    )(*terms, *waited)


def finish(early, late, scale):
    count = late.shape[1]

    def body(first, second, out):
        lane = lax.broadcasted_iota(jnp.int32, (OWNERS * LATE, BS), 1)
        head = sum((first[s] for s in range(1, first.shape[0])), first[0]) * scale
        for w in range(count):
            rest = sum((second[s, w] for s in range(1, second.shape[0])), second[0, w]) * scale
            if w == 0:
                top = head[:EARLY]
            else:
                last = jnp.zeros((8, BS), jnp.float32)
                for q in range(EARLY // 8):
                    moved = pltpu.roll(head[8 * q:8 * q + 8], (LA * q - EA) % BS, 1)
                    last = jnp.where(lane[:8] // LA == q, moved, last)
                top = jnp.concatenate([head[EARLY:], last], axis=0)
            packed = rest[LATE:]
            stacked = jnp.concatenate(
                [packed if q == 0 else pltpu.roll(packed, BS - q * EARLY, 1) for q in range(OWNERS)], axis=0
            )
            turned = jnp.concatenate([stacked] * (BS // (OWNERS * LATE)), axis=0).T
            rows = jnp.concatenate(
                [
                    jnp.where(lane[:EARLY] < EA, top, turned[:EARLY]),
                    rest[:LATE],
                ],
                axis=0,
            )
            result = jnp.zeros((EARLY + LATE, BS), jnp.float32)
            for o in range(OWNERS):
                at = o * (EARLY + LATE)
                for low, size, source in ((at, EARLY, o * EARLY), (at + EARLY, LATE, EA + o * LATE)):
                    by = (low - source) % BS
                    moved = pltpu.roll(rows, by, 1) if by else rows
                    result = jnp.where((lane >= low) & (lane < low + size), moved, result)
            out[w] = result

    return pl.pallas_call(
        body,
        out_shape=jax.ShapeDtypeStruct((count, EARLY + LATE, BS), jnp.float32),
        compiler_params=room(16),
        cost_estimate=SMALL,
        name="finish",
    )(early, late)


def on_device(jac, obs_group, group_weight, pattern, pairs):
    total_obs = jac.shape[1] * NX
    core = lax.axis_index("c").astype(jnp.int32).reshape(1)
    listed = pairs.reshape(-1)
    choice = obs_group[0][None, :] == jnp.arange(group_weight.shape[0], dtype=jnp.int32)[:, None]
    root = jnp.sum(jnp.where(choice, group_weight[:, None], 0.0), axis=0)
    factors = pattern[0, 0].astype(jnp.float32)[:, None] * root[None, :]

    early = lax.all_to_all(relayout(jac, 0, EARLY), OBS_AXES, 0, 0, tiled=True)
    late = lax.all_to_all(relayout(jac, EARLY, LATE), OBS_AXES, 0, 0, tiled=True)

    give, keep, kept = early_tiles(early, factors, listed, core)
    kept = kept.reshape(2, NB, EA, -1)
    parts = total("x", [keep, swap_cores(give)], [])
    keep, *gives = late_tiles(late, kept, factors, listed, core, *parts)
    parts = total("y", send_on("x", parts), [])
    rest = total("x", [keep], [swap_cores(give) for give in gives], *parts)
    parts = merge(send_on("y", parts))
    parts = lax.all_to_all(parts, "z", 0, 0, tiled=True)
    rest = merge(send_on("x", rest), parts).reshape(NZ * NY, 2, 2 * LATE, BS)
    rest = lax.all_to_all(rest, ("z", "y"), 0, 0, tiled=True)
    return finish(parts, rest, 1.0 / math.sqrt(total_obs))


def solution(mesh):
    fine = Mesh(mesh.devices.reshape(NZ, NY, NC, NX), ("z", "y", "c", "x"))
    return jax.shard_map(
        on_device,
        mesh=fine,
        in_specs=(P(OBS_AXES, "x"), P("x", OBS_AXES), P(), P("x", OBS_AXES, None), P()),
        out_specs=P(OBS_AXES, "x", None),
        check_vma=False,
    )
```

```python
import math

import jax
import jax.numpy as jnp
from jax import lax
from jax.experimental import pallas as pl
from jax.experimental.pallas import tpu as pltpu
from jax.sharding import Mesh, PartitionSpec as P

NZ, NY, NC, NX = 8, 4, 2, 4
PARTS = NZ * NY * NC
OBS_AXES = ("z", "y", "c")
NB, BS = 16, 128
OWNERS = 4
EARLY, LATE = 24, 8
EA, LA = OWNERS * EARLY, OWNERS * LATE
PACKED = 2 * EARLY - 8
ANYWHERE = pl.BlockSpec(memory_space=pl.ANY)
SMALL = pl.CostEstimate(flops=1, bytes_accessed=1, transcendentals=0)


def room(mebibytes):
    return pltpu.CompilerParams(vmem_limit_bytes=mebibytes * 2**20)


def relayout(jac, start, rows):
    width = jac.shape[1] // PARTS

    loads = 8
    span = PARTS // loads

    def body(src, out, hold, sems):
        copies = []
        for n in range(loads):
            lanes = pl.ds(n * span * width, span * width)
            copies.append(pltpu.make_async_copy(src.at[pl.ds(start, rows), lanes], hold.at[:, lanes], sems.at[n]))
            copies[-1].start()
        stores = []
        for n in range(loads):
            copies[n].wait()
            for i in range(n * span, (n + 1) * span):
                lanes = pl.ds(i * width, width)
                stores.append(pltpu.make_async_copy(hold.at[:, lanes], out.at[i], sems.at[loads + i]))
                stores[-1].start()
        for store in stores:
            store.wait()

    return pl.pallas_call(
        body,
        in_specs=[ANYWHERE],
        out_specs=ANYWHERE,
        out_shape=jax.ShapeDtypeStruct((PARTS, rows, width), jac.dtype),
        scratch_shapes=[
            pltpu.VMEM((rows, PARTS * width), jac.dtype),
            pltpu.SemaphoreType.DMA((loads + PARTS,)),
        ],
        compiler_params=room(60),
        cost_estimate=SMALL,
        name="relayout",
    )(jac)


def dot(u, v):
    return lax.dot_general(u, v, (((1,), (1,)), ((), ())), preferred_element_type=jnp.float32)


def split(value):
    top = value.astype(jnp.bfloat16)
    return top, (value - top.astype(jnp.float32)).astype(jnp.bfloat16)


def each_owner(pairs_ref, mine, store, first=0, count=NZ):
    def one(s, carry):
        z, y = first + s // NY, s % NY
        k = ((z * NY + y) * NC + mine) * 2
        store(z, y, [(pairs_ref[2 * k + 2 * w], pairs_ref[2 * k + 2 * w + 1]) for w in range(2)])
        return carry

    lax.fori_loop(0, count * NY, one, 0, unroll=4)


def early_tiles(received, factors, pairs, core):
    width = received.shape[-1]
    pieces = 8
    held = PARTS // pieces
    total = NB * EA
    tall = 256

    def body(pairs_ref, core_ref, fac, src, give, keep, kept, arrived, halves, prod, out, sems):
        loads = [
            pltpu.make_async_copy(
                src.at[pl.ds(p * held, held)], arrived.at[pl.ds(p * held, held)], sems.at[p]
            )
            for p in range(pieces)
        ]
        for load in loads:
            load.start()
        lane = lax.broadcasted_iota(jnp.int32, (tall, BS), 1)

        def convert(i, carry):
            value = arrived[pl.ds(i * OWNERS, OWNERS)].reshape(EA, width) * fac[pl.ds(i, 1), :]
            rows = pl.ds(pl.multiple_of(i * EA, EA), EA)
            halves[0, rows, :], halves[1, rows, :] = split(value)
            return carry

        def place(rows, start, value):
            stop = start + value.shape[1]
            for j in range(start // EA, -(-stop // EA)):
                low, high = max(j * EA, start), min((j + 1) * EA, stop)
                by = (start - j * EA) % BS
                moved = None
                for t in range((low - start) // BS, (high - start - 1) // BS + 1):
                    part = value[:, t * BS:(t + 1) * BS]
                    part = pltpu.roll(part, by, 1) if by else part
                    moved = part if moved is None else jnp.where(lane < start + t * BS - j * EA, moved, part)
                block = slice(j * BS, (j + 1) * BS)
                if low > j * EA:
                    moved = jnp.where(lane < low - j * EA, prod[rows, block], moved)
                prod[rows, block] = moved

        ready = 0
        for g in range(total // tall):
            while ready * held * EARLY < (g + 1) * tall:
                loads[ready].wait()
                lax.fori_loop(ready * held // OWNERS, (ready + 1) * held // OWNERS, convert, 0)
                ready += 1
            cols = slice(g * tall, (g + 1) * tall)

            def row(a, carry, cols=cols, g=g):
                rows = pl.ds(pl.multiple_of(a * tall, tall), tall)
                ah, al = halves[0, rows, :], halves[1, rows, :]
                bh, bl = halves[0, cols, :], halves[1, cols, :]
                place(rows, g * tall, dot(ah, bh) + (dot(ah, bl) + dot(al, bh)))
                return carry

            lax.fori_loop(0, g + 1, row, 0)
            if g * tall % EA:
                rows = slice(g * tall, g * tall + 64)
                cols = slice(g * tall // EA * EA, g * tall)
                ah, al = halves[0, rows, :], halves[1, rows, :]
                bh, bl = halves[0, cols, :], halves[1, cols, :]
                value = dot(ah, bh) + (dot(ah, bl) + dot(al, bh))
                at = g * tall // EA * BS
                prod[rows, at:at + value.shape[1]] = value

        save = pltpu.make_async_copy(halves, kept, sems.at[pieces])
        save.start()
        sends = []

        for n, (dst, who) in enumerate(((give, 1 - core_ref[0]), (keep, core_ref[0]))):

            def store(z, y, pairs, n=n):
                tiles = []
                for i, j in pairs:
                    rows = pl.multiple_of(i * EA, EA)
                    cols = pl.ds(pl.multiple_of(j * BS, BS), BS)
                    tiles.append([prod[pl.ds(rows + x * EARLY, EARLY), cols] for x in range(NX)])
                for x in range(NX):
                    head, tail = tiles[0][x], tiles[1][x]
                    last = tail[EARLY - 8:]
                    gaps = [pltpu.roll(last, EA - LA * q, 1) for q in range(EARLY // 8)]
                    out[n, x, y, z, 0:EARLY] = jnp.where(lane[:EARLY] < EA, head, jnp.concatenate(gaps, axis=0))
                    out[n, x, y, z, EARLY:PACKED] = tail[:EARLY - 8]

            for h in range(2):
                zs = pl.ds(h * NZ // 2, NZ // 2)
                each_owner(pairs_ref, who, store, h * NZ // 2, NZ // 2)
                sends.append(
                    pltpu.make_async_copy(
                        out.at[n, :, :, zs], dst.at[:, :, zs], sems.at[pieces + 1 + 2 * n + h]
                    )
                )
                sends[-1].start()
        for send in sends:
            send.wait()
        save.wait()

    shape = (NX, NY, NZ, PACKED, BS)
    return pl.pallas_call(
        body,
        grid_spec=pltpu.PrefetchScalarGridSpec(
            num_scalar_prefetch=2,
            grid=(1,),
            in_specs=[pl.BlockSpec(factors.shape, lambda i, *_: (0, 0)), ANYWHERE],
            out_specs=[ANYWHERE] * 3,
            scratch_shapes=[
                pltpu.VMEM(received.shape, jnp.float32),
                pltpu.VMEM((2, total, width), jnp.bfloat16),
                pltpu.VMEM((total, NB * BS), jnp.float32),
                pltpu.VMEM((2,) + shape, jnp.float32),
                pltpu.SemaphoreType.DMA((pieces + 5,)),
            ],
        ),
        out_shape=[jax.ShapeDtypeStruct(shape, jnp.float32)] * 2
        + [jax.ShapeDtypeStruct((2, total, width), jnp.bfloat16)],
        compiler_params=room(58),
        cost_estimate=pl.CostEstimate(flops=10**11, bytes_accessed=18 * 2**20, transcendentals=0),
        name="early_tiles",
    )(pairs, core, factors, received)


def late_tiles(received, kept, factors, pairs, core, *waited):
    width = received.shape[-1]

    def body(pairs_ref, core_ref, src, fac, kept_ref, *refs):
        refs = refs[len(waited):]
        keep, gives = refs[0], refs[1:1 + NX]
        halves, late, prod, out, sems = refs[1 + NX:]
        loads = [
            pltpu.make_async_copy(
                kept_ref.at[:, pl.ds(2 * g, 2)], halves.at[:, pl.ds(2 * g, 2), pl.ds(0, EA), :], sems.at[g]
            )
            for g in range(NB // 2)
        ]
        for load in loads:
            load.start()

        def convert(i, carry):
            value = src[pl.ds(i * OWNERS, OWNERS)].reshape(LA, width) * fac[pl.ds(i, 1), :]
            rows = pl.ds(pl.multiple_of(i * LA, LA), LA)
            for part, half in enumerate(split(value)):
                halves[part, i, EA:BS, :] = half
                late[part, rows, :] = half
            return carry

        lax.fori_loop(0, NB, convert, 0)

        def column(g, carry):
            for h in range(NB // 4):

                @pl.when(g == h)
                def _(h=h):
                    loads[2 * h].wait()
                    loads[2 * h + 1].wait()

            bh, bl = (halves[part, pl.ds(4 * g, 4)].reshape(4 * BS, width) for part in (0, 1))
            ah, al = late[0], late[1]
            cols = pl.ds(pl.multiple_of(g * 512, 512), 512)
            prod[:, cols] = dot(ah, bh) + (dot(ah, bl) + dot(al, bh))
            return carry

        lax.fori_loop(0, NB // 4, column, 0)
        lane = lax.broadcasted_iota(jnp.int32, (LATE, BS), 1)
        masks = {far: (lane // (far * EARLY)) % 2 == 0 for far in (2, 1)}

        sends = []

        for n, who in enumerate((1 - core_ref[0], core_ref[0])):

            def store(z, y, pairs, n=n):
                for w, (i, j) in enumerate(pairs):
                    part = prod[pl.ds(pl.multiple_of(i * LA, LA), LA), pl.ds(pl.multiple_of(j * BS, BS), BS)]
                    flip = prod[pl.ds(pl.multiple_of(j * LA, LA), LA), pl.ds(pl.multiple_of(i * BS, BS), BS)]
                    turn = [flip[q * LATE:(q + 1) * LATE] for q in range(OWNERS)]
                    for far in (2, 1):
                        by = far * EARLY
                        for q in range(OWNERS):
                            if q & far == 0:
                                u, v = turn[q], turn[q | far]
                                turn[q] = jnp.where(masks[far], u, pltpu.roll(v, by, 1))
                                turn[q | far] = jnp.where(masks[far], pltpu.roll(u, BS - by, 1), v)
                    for x in range(NX):
                        out[n, x, z, y, w, 0:LATE] = part[x * LATE:(x + 1) * LATE]
                        out[n, x, z, y, w, LATE:2 * LATE] = turn[x]

            each_owner(pairs_ref, who, store)
            for x in range(NX):
                dst = keep.at[x] if n else gives[x]
                sends.append(pltpu.make_async_copy(out.at[n, x], dst, sems.at[NB // 2 + n * NX + x]))
                sends[-1].start()
        for send in sends:
            send.wait()

    shape = (NX, NZ, NY, 2, 2 * LATE, BS)
    whole = lambda shape: pl.BlockSpec(shape, lambda i, *_: (0,) * len(shape))
    return pl.pallas_call(
        body,
        grid_spec=pltpu.PrefetchScalarGridSpec(
            num_scalar_prefetch=2,
            grid=(1,),
            in_specs=[whole(received.shape), whole(factors.shape)] + [ANYWHERE] * (1 + len(waited)),
            out_specs=[ANYWHERE] * (1 + NX),
            scratch_shapes=[
                pltpu.VMEM((2, NB, BS, width), jnp.bfloat16),
                pltpu.VMEM((2, NB * LA, width), jnp.bfloat16),
                pltpu.VMEM((NB * LA, NB * BS), jnp.float32),
                pltpu.VMEM((2,) + shape, jnp.float32),
                pltpu.SemaphoreType.DMA((NB // 2 + 2 * NX,)),
            ],
        ),
        out_shape=[jax.ShapeDtypeStruct(shape, jnp.float32)]
        + [jax.ShapeDtypeStruct(shape[1:], jnp.float32)] * NX,
        compiler_params=room(58),
        cost_estimate=pl.CostEstimate(flops=10**11, bytes_accessed=12 * 2**20, transcendentals=0),
        name="late_tiles",
    )(pairs, core, received, factors, kept, *waited)


def swap_cores(value):
    return lax.ppermute(value, "c", [(0, 1), (1, 0)])


def total(axis, wholes, pieces, *waited):
    size = wholes[0].shape[0]
    shape = wholes[0].shape[1:]
    place = lax.axis_index(axis).astype(jnp.int32).reshape(1)

    def body(place_ref, *refs):
        whole_refs = refs[:len(wholes)]
        piece_refs = refs[len(wholes):len(wholes) + len(pieces)]
        outs = refs[len(refs) - size:]
        for d in range(size):
            at = lax.rem(place_ref[0] + d, size)
            for s in range(size):

                @pl.when(at == s)
                def _(d=d, s=s):
                    value = whole_refs[0][s]
                    for ref in whole_refs[1:]:
                        value = value + ref[s]
                    if pieces:
                        value = value + piece_refs[s][...]
                    outs[d][...] = value

    tail = (0,) * (len(shape) - 1)
    cut = (shape[0] // 2,) + shape[1:]
    full = pl.BlockSpec((size,) + cut, lambda i, *_: (0, i) + tail)
    part = pl.BlockSpec(cut, lambda i, *_: (i,) + tail)
    return pl.pallas_call(
        body,
        grid_spec=pltpu.PrefetchScalarGridSpec(
            num_scalar_prefetch=1,
            grid=(2,),
            in_specs=[full] * len(wholes) + [part] * len(pieces) + [ANYWHERE] * len(waited),
            out_specs=[part] * size,
        ),
        out_shape=[jax.ShapeDtypeStruct(shape, jnp.float32)] * size,
        compiler_params=room(16),
        cost_estimate=SMALL,
        name="total",
    )(place, *wholes, *pieces, *waited)


def send_on(axis, parts):
    size = len(parts)
    return [parts[0]] + [
        lax.ppermute(parts[d], axis, [(s, (s + d) % size) for s in range(size)]) for d in range(1, size)
    ]


def merge(terms, *waited):
    def body(*refs):
        value = refs[0][...]
        for ref in refs[1:len(terms)]:
            value = value + ref[...]
        refs[-1][...] = value

    vmem = pl.BlockSpec(memory_space=pltpu.VMEM)
    return pl.pallas_call(
        body,
        in_specs=[vmem] * len(terms) + [ANYWHERE] * len(waited),
        out_specs=vmem,
        out_shape=jax.ShapeDtypeStruct(terms[0].shape, jnp.float32),
        compiler_params=room(16),
        cost_estimate=SMALL,
        name="merge",
    )(*terms, *waited)


def finish(early, late, scale):
    count = late.shape[1]

    def body(first, second, out):
        lane = lax.broadcasted_iota(jnp.int32, (OWNERS * LATE, BS), 1)
        head = sum((first[s] for s in range(1, first.shape[0])), first[0]) * scale
        for w in range(count):
            rest = sum((second[s, w] for s in range(1, second.shape[0])), second[0, w]) * scale
            if w == 0:
                top = head[:EARLY]
            else:
                last = jnp.zeros((8, BS), jnp.float32)
                for q in range(EARLY // 8):
                    moved = pltpu.roll(head[8 * q:8 * q + 8], (LA * q - EA) % BS, 1)
                    last = jnp.where(lane[:8] // LA == q, moved, last)
                top = jnp.concatenate([head[EARLY:], last], axis=0)
            packed = rest[LATE:]
            stacked = jnp.concatenate(
                [packed if q == 0 else pltpu.roll(packed, BS - q * EARLY, 1) for q in range(OWNERS)], axis=0
            )
            turned = jnp.concatenate([stacked] * (BS // (OWNERS * LATE)), axis=0).T
            rows = jnp.concatenate(
                [
                    jnp.where(lane[:EARLY] < EA, top, turned[:EARLY]),
                    rest[:LATE],
                ],
                axis=0,
            )
            result = jnp.zeros((EARLY + LATE, BS), jnp.float32)
            for o in range(OWNERS):
                at = o * (EARLY + LATE)
                for low, size, source in ((at, EARLY, o * EARLY), (at + EARLY, LATE, EA + o * LATE)):
                    by = (low - source) % BS
                    moved = pltpu.roll(rows, by, 1) if by else rows
                    result = jnp.where((lane >= low) & (lane < low + size), moved, result)
            out[w] = result

    return pl.pallas_call(
        body,
        out_shape=jax.ShapeDtypeStruct((count, EARLY + LATE, BS), jnp.float32),
        compiler_params=room(16),
        cost_estimate=SMALL,
        name="finish",
    )(early, late)


def on_device(jac, obs_group, group_weight, pattern, pairs):
    total_obs = jac.shape[1] * NX
    core = lax.axis_index("c").astype(jnp.int32).reshape(1)
    listed = pairs.reshape(-1)
    choice = obs_group[0][None, :] == jnp.arange(group_weight.shape[0], dtype=jnp.int32)[:, None]
    root = jnp.sum(jnp.where(choice, group_weight[:, None], 0.0), axis=0)
    factors = pattern[0, 0].astype(jnp.float32)[:, None] * root[None, :]

    early = lax.all_to_all(relayout(jac, 0, EARLY), OBS_AXES, 0, 0, tiled=True)
    late = lax.all_to_all(relayout(jac, EARLY, LATE), OBS_AXES, 0, 0, tiled=True)

    give, keep, kept = early_tiles(early, factors, listed, core)
    kept = kept.reshape(2, NB, EA, -1)
    parts = total("x", [keep, swap_cores(give)], [])
    keep, *gives = late_tiles(late, kept, factors, listed, core, *parts[1:])
    parts = total("y", send_on("x", parts), [])
    rest = total("x", [keep], [swap_cores(give) for give in gives], *parts)
    parts = merge(send_on("y", parts))
    parts = lax.all_to_all(parts, "z", 0, 0, tiled=True)
    rest = merge(send_on("x", rest), parts).reshape(NZ * NY, 2, 2 * LATE, BS)
    rest = lax.all_to_all(rest, ("z", "y"), 0, 0, tiled=True)
    return finish(parts, rest, 1.0 / math.sqrt(total_obs))


def solution(mesh):
    fine = Mesh(mesh.devices.reshape(NZ, NY, NC, NX), ("z", "y", "c", "x"))
    return jax.shard_map(
        on_device,
        mesh=fine,
        in_specs=(P(OBS_AXES, "x"), P("x", OBS_AXES), P(), P("x", OBS_AXES, None), P()),
        out_specs=P(OBS_AXES, "x", None),
        check_vma=False,
    )
```
